32 devices in a mesh: dp: 32 (over z, y, x, core).
Axes of the slice: x: 2, y: 2, z: 4, core: 2. Of those that a mesh axis runs over, the one named last changes fastest.
Arguments:
- inputs: bfloat16 [64, 1024, 576], P('dp'), may hold values from -6 to 6
- cotangent: bfloat16 [64, 1024, 576], P('dp'), may hold values from -6 to 6
- segments: int32 [64, 1024], P('dp'), may hold values from 0 to 2, as said below
- norm_gains: float32 [2, 576], replicated, may hold values from 0.5 to 1.5
- query_weight: float32 [331776], P('dp'), may hold values from -0.25 to 0.25
- key_weight: float32 [110592], P('dp'), may hold values from -0.25 to 0.25
- value_weight: float32 [110592], P('dp'), may hold values from -0.25 to 0.25
- out_weight: float32 [331776], P('dp'), may hold values from -0.75 to 0.75
- gate_weight: float32 [884736], P('dp'), may hold values from -0.25 to 0.25
- up_weight: float32 [884736], P('dp'), may hold values from -0.25 to 0.25
- down_weight: float32 [884736], P('dp'), may hold values from -0.15625 to 0.15625
- query_first: float32 [331776], P('dp'), may hold values from -256 to 256
- key_first: float32 [110592], P('dp'), may hold values from -256 to 256
- value_first: float32 [110592], P('dp'), may hold values from -256 to 256
- out_first: float32 [331776], P('dp'), may hold values from -64 to 64
- gate_first: float32 [884736], P('dp'), may hold values from -64 to 64
- up_first: float32 [884736], P('dp'), may hold values from -64 to 64
- down_first: float32 [884736], P('dp'), may hold values from -96 to 96
- query_second: float32 [331776], P('dp'), may hold values from 7864.32 to 31457.28
- key_second: float32 [110592], P('dp'), may hold values from 7864.32 to 31457.28
- value_second: float32 [110592], P('dp'), may hold values from 7864.32 to 31457.28
- out_second: float32 [331776], P('dp'), may hold values from 458.752 to 1835.008
- gate_second: float32 [884736], P('dp'), may hold values from 458.752 to 1835.008
- up_second: float32 [884736], P('dp'), may hold values from 458.752 to 1835.008
- down_second: float32 [884736], P('dp'), may hold values from 1245.184 to 4980.736
- gain_first: float32 [2, 576], replicated, may hold values from -224 to 224
- gain_second: float32 [2, 576], replicated, may hold values from 2621.44 to 13107.2
Outputs:
- outputs: bfloat16 [64, 1024, 576], P('dp')
- input_grad: float32 [64, 1024, 576], P('dp')
- query_grad: float32 [331776], P('dp')
- query_moment: float32 [331776], P('dp')
- query_new: float32 [331776], P('dp')
- key_grad: float32 [110592], P('dp')
- key_moment: float32 [110592], P('dp')
- key_new: float32 [110592], P('dp')
- value_grad: float32 [110592], P('dp')
- value_moment: float32 [110592], P('dp')
- value_new: float32 [110592], P('dp')
- out_grad: float32 [331776], P('dp')
- out_moment: float32 [331776], P('dp')
- out_new: float32 [331776], P('dp')
- gate_grad: float32 [884736], P('dp')
- gate_moment: float32 [884736], P('dp')
- gate_new: float32 [884736], P('dp')
- up_grad: float32 [884736], P('dp')
- up_moment: float32 [884736], P('dp')
- up_new: float32 [884736], P('dp')
- down_grad: float32 [884736], P('dp')
- down_moment: float32 [884736], P('dp')
- down_new: float32 [884736], P('dp')
- gain_grad: float32 [2, 576], replicated
- gain_moment: float32 [2, 576], replicated
- gains_new: float32 [2, 576], replicated
The draws below stay inside these ranges and needn't reach their ends.
Inputs may be any that keep to these rules, and one draw needn't show every extreme that they name: `segments`: in each sequence the segment numbers start at 0, never fall, and rise by one at each of two places: the first segment holds 64 to 511 tokens, the second 1024 // 5 to 511.
All inputs are finite; a program needn't handle non-finite values.
Results may differ from the reference program's by a relative error of at most 0.013.
Values may be sent and summed in bfloat16 or wider, within the bound.
A program may use at most 320 MiB of HBM per device.

```python
import math
import jax
import jax.numpy as jnp
from jax import lax

D = 576
HEADS = 9
KV_HEADS = 3
HEAD = 64
FF = 1536
SEQ = 1024
STEP = 10
SEQS = 64
TOKENS = 65536


def draw_segments(key, part):
    key = jax.random.fold_in(key, 11)
    first_key, second_key = jax.random.split(key)
    first_cut = jax.random.randint(first_key, (SEQS, 1), SEQ // 16, SEQ // 2)
    second_cut = first_cut + jax.random.randint(second_key, (SEQS, 1), SEQ // 5, SEQ // 2)
    places = jnp.arange(SEQ, dtype=jnp.int32)[None, :]
    return (places >= first_cut).astype(jnp.int32) + (places >= second_cut).astype(jnp.int32)


def block_levels(stream_key, extent, cuts, least, top_value):
    def one(position, shards_of):
        steps = jax.random.uniform(jax.random.fold_in(jax.random.fold_in(stream_key, 6), position), (shards_of,), jnp.float32, least / len(cuts), top_value / len(cuts))
        return jnp.repeat(jnp.exp(steps), extent[position] // shards_of).reshape((-1,) + (1,) * (len(extent) - position - 1))

    loudness = one(*cuts[0])
    for cut in cuts[1:]:
        loudness = loudness * one(*cut)
    return loudness


def gaussian(own_key, extent, deviation, most, cuts=(), held_as=jnp.bfloat16):
    values = jax.random.normal(own_key, extent, jnp.float32) * deviation
    if len(cuts) > 0:
        values = block_levels(own_key, extent, cuts, -0.22, 0.18) * values
    return jnp.clip(values, min=-most, max=most).astype(held_as)


def setup_inputs(seed: int = 0) -> dict:
    key_list = jax.random.split(jax.random.key(seed), 28)
    inputs = gaussian(key_list[0], (SEQS, SEQ, D), 1.0, 6.0, ((0, 32),))
    cotangent = gaussian(key_list[1], (SEQS, SEQ, D), 1.0, 6.0, ((0, 32),))
    segments = draw_segments(jax.random.fold_in(key_list[27], 71), 0)
    norm_gains = jnp.clip(1.0 + 0.1 * jax.random.normal(key_list[3], (2, D), jnp.float32), 0.5, 1.5)
    query_weight = gaussian(key_list[4], (D * HEADS * HEAD,), D ** -0.5, 0.25, ((0, 32),), jnp.float32)
    key_weight = gaussian(key_list[5], (D * KV_HEADS * HEAD,), D ** -0.5, 0.25, ((0, 32),), jnp.float32)
    value_weight = gaussian(key_list[6], (D * KV_HEADS * HEAD,), D ** -0.5, 0.25, ((0, 32),), jnp.float32)
    out_weight = gaussian(key_list[7], (HEADS * HEAD * D,), (HEADS * HEAD // 9) ** -0.5, 0.75, ((0, 32),), jnp.float32)
    gate_weight = gaussian(key_list[8], (D * FF,), D ** -0.5, 0.25, ((0, 32),), jnp.float32)
    up_weight = gaussian(key_list[9], (D * FF,), D ** -0.5, 0.25, ((0, 32),), jnp.float32)
    down_weight = gaussian(key_list[10], (FF * D,), FF ** -0.5, 0.15625, ((0, 32),), jnp.float32)
    query_first = gaussian(key_list[11], (D * HEADS * HEAD,), (0.17 * TOKENS ** 0.5), 256.0, ((0, 32),), jnp.float32)
    key_first = gaussian(key_list[12], (D * KV_HEADS * HEAD,), (0.17 * TOKENS ** 0.5), 256.0, ((0, 32),), jnp.float32)
    value_first = gaussian(key_list[13], (D * KV_HEADS * HEAD,), (0.17 * TOKENS ** 0.5), 256.0, ((0, 32),), jnp.float32)
    out_first = gaussian(key_list[14], (HEADS * HEAD * D,), (0.04 * TOKENS ** 0.5), 64.0, ((0, 32),), jnp.float32)
    gate_first = gaussian(key_list[15], (D * FF,), (0.04 * TOKENS ** 0.5), 64.0, ((0, 32),), jnp.float32)
    up_first = gaussian(key_list[16], (D * FF,), (0.04 * TOKENS ** 0.5), 64.0, ((0, 32),), jnp.float32)
    down_first = gaussian(key_list[17], (FF * D,), (0.067 * TOKENS ** 0.5), 96.0, ((0, 32),), jnp.float32)
    query_second = jnp.clip(jnp.exp(math.log(31457.28) - 1.3862944 * jax.random.uniform(key_list[18], (D * HEADS * HEAD,), jnp.float32) ** block_levels(key_list[18], (D * HEADS * HEAD,), ((0, 32),), -0.2, 0.2)), 7864.32, 31457.28)
    key_second = jnp.clip(jnp.exp(math.log(31457.28) - 1.3862944 * jax.random.uniform(key_list[19], (D * KV_HEADS * HEAD,), jnp.float32) ** block_levels(key_list[19], (D * KV_HEADS * HEAD,), ((0, 32),), -0.2, 0.2)), 7864.32, 31457.28)
    value_second = jnp.clip(jnp.exp(math.log(31457.28) - 1.3862944 * jax.random.uniform(key_list[20], (D * KV_HEADS * HEAD,), jnp.float32) ** block_levels(key_list[20], (D * KV_HEADS * HEAD,), ((0, 32),), -0.2, 0.2)), 7864.32, 31457.28)
    out_second = jnp.clip(jnp.exp(math.log(1835.008) - 1.3862944 * jax.random.uniform(key_list[21], (HEADS * HEAD * D,), jnp.float32) ** block_levels(key_list[21], (HEADS * HEAD * D,), ((0, 32),), -0.2, 0.2)), 458.752, 1835.008)
    gate_second = jnp.clip(jnp.exp(math.log(1835.008) - 1.3862944 * jax.random.uniform(key_list[22], (D * FF,), jnp.float32) ** block_levels(key_list[22], (D * FF,), ((0, 32),), -0.2, 0.2)), 458.752, 1835.008)
    up_second = jnp.clip(jnp.exp(math.log(1835.008) - 1.3862944 * jax.random.uniform(key_list[23], (D * FF,), jnp.float32) ** block_levels(key_list[23], (D * FF,), ((0, 32),), -0.2, 0.2)), 458.752, 1835.008)
    down_second = jnp.clip(jnp.exp(math.log(4980.736) - 1.3862944 * jax.random.uniform(key_list[24], (FF * D,), jnp.float32) ** block_levels(key_list[24], (FF * D,), ((0, 32),), -0.2, 0.2)), 1245.184, 4980.736)
    gain_first = gaussian(key_list[25], (2, D), (0.15 * TOKENS ** 0.5), 224.0, (), jnp.float32)
    gain_second = jnp.clip(jnp.exp(jax.random.uniform(key_list[26], (2, D), jnp.float32, math.log(2621.44), math.log(13107.2))), 2621.44, 13107.2)
    return {"inputs": inputs, "cotangent": cotangent, "segments": segments, "norm_gains": norm_gains, "query_weight": query_weight, "key_weight": key_weight, "value_weight": value_weight, "out_weight": out_weight, "gate_weight": gate_weight, "up_weight": up_weight, "down_weight": down_weight, "query_first": query_first, "key_first": key_first, "value_first": value_first, "out_first": out_first, "gate_first": gate_first, "up_first": up_first, "down_first": down_first, "query_second": query_second, "key_second": key_second, "value_second": value_second, "out_second": out_second, "gate_second": gate_second, "up_second": up_second, "down_second": down_second, "gain_first": gain_first, "gain_second": gain_second}


norm_eps = 1e-05
rope_base = 100000.0
learn_rate = 0.06
gain_rate = 0.4
beta_first = 0.9
beta_second = 0.95
adam_eps = 1e-08
decay_rate = 0.1

@jax.custom_vjp
def low(v):
    return lax.optimization_barrier(v.astype(jnp.bfloat16)).astype(jnp.float32)

@jax.custom_vjp
def low_back(v):
    return v

def low_keep(v):
    return (low(v), None)

def low_pass(kept, grad):
    return (grad,)

def back_keep(v):
    return (v, None)

def back_low(kept, grad):
    return (low(grad),)
low.defvjp(low_keep, low_pass)
low_back.defvjp(back_keep, back_low)

def rms_scale(values, gain):
    return values * lax.rsqrt(lax.optimization_barrier(jnp.mean(values * values, axis=-1, keepdims=True)) + norm_eps) * gain

def doc_positions(segments):
    places = jnp.arange(segments.shape[-1], dtype=jnp.int32)
    first_col = jnp.ones(segments.shape[:-1] + (1,), dtype=jnp.bool_)
    change = jnp.concatenate([first_col, segments[..., 1:] != segments[..., :-1]], axis=-1)
    starts = lax.cummax(jnp.where(change, places, jnp.zeros_like(places)), axis=segments.ndim - 1)
    return places - starts

def rope_tables(positions):
    half_size = HEAD // 2
    frequency = rope_base ** (-(jnp.arange(half_size, dtype=jnp.float32) * 2.0 / HEAD))
    angles = positions.astype(jnp.float32)[..., None] * frequency
    return (jnp.cos(angles), jnp.sin(angles))

def rotate(values, cosine_part, sine_part):
    half_size = values.shape[-1] // 2
    first_half = values[..., :half_size]
    second_half = values[..., half_size:]
    cos_rows = cosine_part[..., None, :]
    sin_rows = sine_part[..., None, :]
    return jnp.concatenate([first_half * cos_rows - second_half * sin_rows, second_half * cos_rows + first_half * sin_rows], axis=-1)

def project(left, right):
    return jnp.einsum('...i,ij->...j', left, right, precision=lax.Precision.HIGHEST)

def attend_sequence(query_rows, key_rows, value_rows, seg_row):
    block_rows = min(512, SEQ)
    score_scale = HEAD ** (-0.5)
    places = jnp.arange(SEQ, dtype=jnp.int32)
    pieces = []
    for offset in range(0, SEQ, block_rows):
        query_block = query_rows[offset:offset + block_rows]
        raw_scores = low_back(jnp.einsum('qkgd,skd->kgqs', query_block, key_rows, precision=lax.Precision.HIGHEST))
        same_doc = seg_row[offset:offset + block_rows, None] == seg_row[None, :]
        causal = places[offset:offset + block_rows, None] >= places[None, :]
        allowed = jnp.logical_and(same_doc, causal)
        scaled = jnp.where(allowed, raw_scores * score_scale, -1e+30)
        top_score = lax.optimization_barrier(jnp.max(scaled, axis=-1, keepdims=True))
        exp_terms = jnp.where(allowed, jnp.exp(scaled - top_score), 0.0)
        attn_probs = low(exp_terms / lax.optimization_barrier(jnp.sum(exp_terms, axis=-1, keepdims=True)))
        pieces.append(jnp.einsum('kgqs,skd->qkgd', attn_probs, value_rows, precision=lax.Precision.HIGHEST))
    return jnp.concatenate(pieces, axis=0)

def attend_bundle(bundle):
    return attend_sequence(bundle[0], bundle[1], bundle[2], bundle[3])

def forward_group(input_rows, seg_rows, matrices, gain_pair):
    query_mat, key_mat, value_mat, out_mat, gate_mat, up_mat, down_mat = [low(matrix) for matrix in matrices]
    seq_count = input_rows.shape[0]
    cosine_part, sine_part = rope_tables(doc_positions(seg_rows))
    normed = low(rms_scale(input_rows, gain_pair[0]))
    query_lin = low_back(project(normed, query_mat)).reshape(seq_count, SEQ, HEADS, HEAD)
    key_lin = low_back(project(normed, key_mat)).reshape(seq_count, SEQ, KV_HEADS, HEAD)
    value_rows = low(low_back(project(normed, value_mat))).reshape(seq_count, SEQ, KV_HEADS, HEAD)
    query_rows = low(rotate(query_lin, cosine_part, sine_part)).reshape(seq_count, SEQ, KV_HEADS, HEADS // KV_HEADS, HEAD)
    key_rows = low(rotate(key_lin, cosine_part, sine_part))
    mixed = lax.map(jax.checkpoint(attend_bundle), (query_rows, key_rows, value_rows, seg_rows))
    attn_rows = low(low_back(mixed.reshape(seq_count, SEQ, HEADS * HEAD)))
    middle = input_rows + low_back(project(attn_rows, out_mat))
    normed2 = low(rms_scale(middle, gain_pair[1]))
    gate_lin = low_back(project(normed2, gate_mat))
    up_lin = low_back(project(normed2, up_mat))
    hidden = low(jax.nn.silu(gate_lin) * up_lin)
    return middle + low_back(project(hidden, down_mat))

def adam_step(weight_now, gradient, moment_one, moment_two, step_rate, decay_value):
    one_new = beta_first * moment_one + (1.0 - beta_first) * gradient
    two_new = beta_second * moment_two + (1.0 - beta_second) * gradient * gradient
    fix_first = 1.0 - beta_first ** STEP
    fix_second = 1.0 - beta_second ** STEP
    weight_new = weight_now - step_rate * (one_new / fix_first / (jnp.sqrt(two_new / fix_second) + adam_eps) + decay_value * weight_now)
    return (two_new, weight_new)

def reference(inputs, cotangent, segments, norm_gains, query_weight, key_weight, value_weight, out_weight, gate_weight, up_weight, down_weight, query_first, key_first, value_first, out_first, gate_first, up_first, down_first, query_second, key_second, value_second, out_second, gate_second, up_second, down_second, gain_first, gain_second):
    query_cols = HEADS * HEAD
    pair_cols = KV_HEADS * HEAD
    shapes = ((D, query_cols), (D, pair_cols), (D, pair_cols), (query_cols, D), (D, FF), (D, FF), (FF, D))
    masters = (query_weight, key_weight, value_weight, out_weight, gate_weight, up_weight, down_weight)
    firsts = (query_first, key_first, value_first, out_first, gate_first, up_first, down_first)
    seconds = (query_second, key_second, value_second, out_second, gate_second, up_second, down_second)
    matrices = tuple((master.reshape(shape_pair) for master, shape_pair in zip(masters, shapes)))
    group_size = 4 if SEQS % 4 == 0 else 1
    group_count = SEQS // group_size
    input_groups = inputs.astype(jnp.float32).reshape(group_count, group_size, SEQ, D)
    back_groups = cotangent.astype(jnp.float32).reshape(group_count, group_size, SEQ, D)
    seg_groups = segments.reshape(group_count, group_size, SEQ)

    def step_group(totals, bundle):
        input_rows, back_rows, seg_rows = bundle

        def local_forward(rows_in, mats_in, gains_in):
            return forward_group(rows_in, seg_rows, mats_in, gains_in)
        result, pull_back = jax.vjp(local_forward, input_rows, matrices, norm_gains)
        input_back, matrix_back, gain_back = pull_back(back_rows)
        totals = jax.tree.map(jnp.add, totals, (matrix_back, gain_back))
        return (totals, (result.astype(jnp.bfloat16), input_back))
    start_totals = (tuple((jnp.zeros(shape_pair, jnp.float32) for shape_pair in shapes)), jnp.zeros((2, D), jnp.float32))
    totals, (result_groups, input_groups_back) = lax.scan(step_group, start_totals, (input_groups, back_groups, seg_groups))
    matrix_totals, gain_total = totals
    outputs = result_groups.reshape(SEQS, SEQ, D)
    input_grad = input_groups_back.reshape(SEQS, SEQ, D)
    results = [outputs, input_grad]
    for slot_index in range(7):
        gradient = matrix_totals[slot_index].reshape(-1)
        moment_new, weight_new = adam_step(masters[slot_index], gradient, firsts[slot_index], seconds[slot_index], learn_rate, decay_rate)
        results.extend([gradient, moment_new, weight_new])
    gain_moment, gains_new = adam_step(norm_gains, gain_total, gain_first, gain_second, gain_rate, 0.0)
    results.extend([gain_total, gain_moment, gains_new])
    return tuple(results)
```

```python
import functools

import jax
import jax.numpy as jnp
from jax import lax
from jax.experimental import pallas as pl
from jax.experimental.pallas import tpu as pltpu
from jax.sharding import PartitionSpec as P

D = 576
HEADS = 9
KV_HEADS = 3
HEAD = 64
FF = 1536
STEP = 10
BLOCK = 256
VMEM_LIMIT = 58 * 2**20

norm_eps = 1e-05
rope_base = 100000.0
learn_rate = 0.06
gain_rate = 0.4
beta_first = 0.9
beta_second = 0.95
adam_eps = 1e-08
decay_rate = 0.1


def doc_positions(segments):
    places = jnp.arange(segments.shape[-1], dtype=jnp.int32)
    first_col = jnp.ones(segments.shape[:-1] + (1,), dtype=jnp.bool_)
    change = jnp.concatenate([first_col, segments[..., 1:] != segments[..., :-1]], axis=-1)
    starts = lax.cummax(jnp.where(change, places, jnp.zeros_like(places)), axis=segments.ndim - 1)
    return places - starts


def rope_tables(positions):
    half_size = HEAD // 2
    frequency = rope_base ** (-(jnp.arange(half_size, dtype=jnp.float32) * 2.0 / HEAD))
    angles = positions.astype(jnp.float32)[..., None] * frequency
    cosine, sine = jnp.cos(angles), jnp.sin(angles)
    return (
        jnp.concatenate([cosine, cosine], axis=-1),
        jnp.concatenate([-sine, sine], axis=-1),
    )


def dot(left, right, left_dim=1, right_dim=0):
    return lax.dot_general(
        left,
        right,
        (((left_dim,), (right_dim,)), ((), ())),
        preferred_element_type=jnp.float32,
    )


def swap_halves(values):
    half = HEAD // 2
    return jnp.concatenate([values[:, half:], values[:, :half]], axis=1)


def norm_parts(values):
    scale = lax.rsqrt(jnp.mean(values * values, axis=-1, keepdims=True) + norm_eps)
    return scale, values * scale


def norm_back(scale, unit, gain, upstream):
    weighted = gain * upstream
    return scale * (weighted - unit * jnp.mean(weighted * unit, axis=-1, keepdims=True))


def mask_block(bias, seg_col, seg_row, start, length):
    key_seg = seg_col[0, 0:length, :]
    query_seg = seg_row[0, :, start : start + BLOCK]
    key_place = lax.broadcasted_iota(jnp.int32, (length, BLOCK), 0)
    query_place = lax.broadcasted_iota(jnp.int32, (length, BLOCK), 1) + start
    allowed = jnp.logical_and(key_seg == query_seg, key_place <= query_place)
    bias[0:length, :] = jnp.where(allowed, 0.0, -1e30)


def attend_kernel(
    x, gains, seg_col, seg_row, cosine, sine, wq, wk, wv, q_out, k_out, v_out, lse_out, att_out,
    att, bias
):
    seq = x.shape[1]
    _, unit = norm_parts(x[0].astype(jnp.float32))
    normed = (unit * gains[0:1, :]).astype(jnp.bfloat16)
    cos, sin = cosine[0], sine[0]
    q_lin = dot(normed, wq[...])
    for h in range(HEADS):
        part = q_lin[:, h * HEAD : (h + 1) * HEAD]
        turned = (part * cos + swap_halves(part) * sin).astype(jnp.bfloat16)
        q_out[0, h] = turned * jnp.bfloat16(0.125)
    k_lin = dot(normed, wk[...])
    v_lin = dot(normed, wv[...])
    for j in range(KV_HEADS):
        part = k_lin[:, j * HEAD : (j + 1) * HEAD]
        k_out[0, j] = (part * cos + swap_halves(part) * sin).astype(jnp.bfloat16)
        v_out[0, j] = v_lin[:, j * HEAD : (j + 1) * HEAD].astype(jnp.bfloat16)
    for start in range(0, seq, BLOCK):
        length = start + BLOCK
        mask_block(bias, seg_col, seg_row, start, length)

        def head_step(h, carry):
            j = lax.div(h, HEADS // KV_HEADS)
            keys = k_out[0, j, 0:length, :]
            values = v_out[0, j, 0:length, :]
            queries = q_out[0, h, start : start + BLOCK, :]
            scores = dot(keys, queries, 1, 1) + bias[0:length, :]
            top = jnp.max(scores, axis=0, keepdims=True)
            terms = jnp.exp(scores - top)
            total = jnp.sum(terms, axis=0, keepdims=True)
            probs = (terms * (1.0 / total)).astype(jnp.bfloat16)
            lse_out[0, h, :, start : start + BLOCK] = top + jnp.log(total)
            att[h, start : start + BLOCK, :] = dot(probs, values, 0, 0).astype(jnp.bfloat16)
            return carry

        lax.fori_loop(0, HEADS, head_step, 0)
    att_out[0] = jnp.concatenate([att[h] for h in range(HEADS)], axis=1)


def feed_kernel(
    x, att, cot, gains, wo, wg, wu, wd,
    out, mid_back, att_back, do_out, dg_out, du_out, dd_out, gain_out,
    acc_o, acc_g, acc_u, acc_d
):
    step = pl.program_id(0)

    @pl.when(step == 0)
    def _():
        for ref in (acc_o, acc_g, acc_u, acc_d, gain_out):
            ref[...] = jnp.zeros_like(ref)

    gain = gains[1:2, :]
    middle = x[...].astype(jnp.float32) + dot(att[...], wo[...])
    scale, unit = norm_parts(middle)
    normed = (unit * gain).astype(jnp.bfloat16)
    gate = dot(normed, wg[...])
    up = dot(normed, wu[...])
    sig = 1.0 / (1.0 + jnp.exp(-gate))
    sil = gate * sig
    hidden = (sil * up).astype(jnp.bfloat16)
    out[...] = (middle + dot(hidden, wd[...])).astype(jnp.bfloat16)
    back = cot[...]
    acc_d[...] += dot(hidden, back, 0, 0)
    hidden_back = dot(back, wd[...], 1, 1)
    gate_back = (hidden_back * up * sig * (1.0 + gate * (1.0 - sig))).astype(jnp.bfloat16)
    up_back = (hidden_back * sil).astype(jnp.bfloat16)
    acc_g[...] += dot(normed, gate_back, 0, 0)
    acc_u[...] += dot(normed, up_back, 0, 0)
    upstream = dot(gate_back, wg[...], 1, 1) + dot(up_back, wu[...], 1, 1)
    gain_out[...] += jnp.sum(upstream * unit, axis=0, keepdims=True)
    middle_back = back.astype(jnp.float32) + norm_back(scale, unit, gain, upstream)
    mid_back[...] = middle_back
    branch = middle_back.astype(jnp.bfloat16)
    acc_o[...] += dot(att[...], branch, 0, 0)
    att_back[...] = dot(branch, wo[...], 1, 1).astype(jnp.bfloat16)

    @pl.when(step == pl.num_programs(0) - 1)
    def _():
        for ref, acc in ((do_out, acc_o), (dg_out, acc_g), (du_out, acc_u), (dd_out, acc_d)):
            ref[...] = acc[...].astype(jnp.bfloat16)


def attend_back_kernel(
    x, gains, seg_col, seg_row, cosine, sine, wq, wk, wv, q_in, k_in, v_in, lse, att_back, mid_back,
    x_back, dq_out, dk_out, dv_out, gain_out,
    ob, dq, dk, dv, bias, acc_q, acc_k, acc_v
):
    step = pl.program_id(0)
    seq = x.shape[1]

    @pl.when(step == 0)
    def _():
        for ref in (acc_q, acc_k, acc_v, gain_out):
            ref[...] = jnp.zeros_like(ref)

    dk[...] = jnp.zeros_like(dk)
    dv[...] = jnp.zeros_like(dv)
    for h in range(HEADS):
        ob[h] = att_back[0, :, h * HEAD : (h + 1) * HEAD]
    for start in range(0, seq, BLOCK):
        length = start + BLOCK
        mask_block(bias, seg_col, seg_row, start, length)

        def head_step(h, carry):
            j = lax.div(h, HEADS // KV_HEADS)
            keys = k_in[0, j, 0:length, :]
            values = v_in[0, j, 0:length, :]
            queries = q_in[0, h, start : start + BLOCK, :]
            out_back = ob[h, start : start + BLOCK, :]
            scores = dot(keys, queries, 1, 1) + bias[0:length, :]
            probs = jnp.exp(scores - lse[0, h, :, start : start + BLOCK])
            dv[j, 0:length, :] += dot(probs.astype(jnp.bfloat16), out_back)
            weighted = probs * dot(values, out_back, 1, 1)
            delta = jnp.sum(weighted, axis=0, keepdims=True)
            score_back = (weighted - probs * delta).astype(jnp.bfloat16)
            dk[j, 0:length, :] += dot(score_back, queries)
            dq[h, start : start + BLOCK, :] = dot(score_back, keys, 0, 0) * 0.125
            return carry

        lax.fori_loop(0, HEADS, head_step, 0)

    cos, sin = cosine[0], sine[0]

    def turn_back(part):
        return (part * cos - swap_halves(part) * sin).astype(jnp.bfloat16)

    q_back = jnp.concatenate([turn_back(dq[h]) for h in range(HEADS)], axis=1)
    k_back = jnp.concatenate([turn_back(dk[j]) for j in range(KV_HEADS)], axis=1)
    v_back = jnp.concatenate([dv[j].astype(jnp.bfloat16) for j in range(KV_HEADS)], axis=1)
    gain = gains[0:1, :]
    scale, unit = norm_parts(x[0].astype(jnp.float32))
    normed = (unit * gain).astype(jnp.bfloat16)
    acc_q[...] += dot(normed, q_back, 0, 0)
    acc_k[...] += dot(normed, k_back, 0, 0)
    acc_v[...] += dot(normed, v_back, 0, 0)
    upstream = (
        dot(q_back, wq[...], 1, 1) + dot(k_back, wk[...], 1, 1) + dot(v_back, wv[...], 1, 1)
    )
    gain_out[...] += jnp.sum(upstream * unit, axis=0, keepdims=True)
    x_back[0] = mid_back[0] + norm_back(scale, unit, gain, upstream)

    @pl.when(step == pl.num_programs(0) - 1)
    def _():
        for ref, acc in ((dq_out, acc_q), (dk_out, acc_k), (dv_out, acc_v)):
            ref[...] = acc[...].astype(jnp.bfloat16)


def whole(shape):
    return pl.BlockSpec(shape, lambda i: (0,) * len(shape))


def per_step(shape):
    return pl.BlockSpec((1,) + shape[1:], lambda i: (i,) + (0,) * (len(shape) - 1))


def sds(shape, dtype):
    return jax.ShapeDtypeStruct(shape, dtype)


def params():
    return pltpu.CompilerParams(
        dimension_semantics=("arbitrary",), vmem_limit_bytes=VMEM_LIMIT
    )


def attention_forward(x, gains, seg_col, seg_row, cosine, sine, wq, wk, wv):
    seqs, seq = x.shape[0], x.shape[1]
    outs = [
        ((seqs, HEADS, seq, HEAD), jnp.bfloat16),
        ((seqs, KV_HEADS, seq, HEAD), jnp.bfloat16),
        ((seqs, KV_HEADS, seq, HEAD), jnp.bfloat16),
        ((seqs, HEADS, 1, seq), jnp.float32),
        ((seqs, seq, D), jnp.bfloat16),
    ]
    return pl.pallas_call(
        attend_kernel,
        grid=(seqs,),
        out_shape=[sds(*o) for o in outs],
        in_specs=[per_step(x.shape), whole(gains.shape)]
        + [per_step(a.shape) for a in (seg_col, seg_row, cosine, sine)]
        + [whole(w.shape) for w in (wq, wk, wv)],
        out_specs=[per_step(o[0]) for o in outs],
        scratch_shapes=[
            pltpu.VMEM((HEADS, seq, HEAD), jnp.bfloat16),
            pltpu.VMEM((seq, BLOCK), jnp.float32),
        ],
        compiler_params=params(),
        cost_estimate=pl.CostEstimate(
            flops=60 * 10**9, bytes_accessed=20 * 10**6, transcendentals=2 * 10**7
        ),
        name="attention_forward",
    )(x, gains, seg_col, seg_row, cosine, sine, wq, wk, wv)


def feed_forward(x, att, cot, gains, wo, wg, wu, wd):
    tokens = x.shape[0]
    rows = pl.BlockSpec((BLOCK, D), lambda i: (i, 0))
    fixed = lambda shape: pl.BlockSpec(shape, lambda i: (0, 0), pipeline_mode=pl.Buffered(1))
    weights = (wo, wg, wu, wd)
    return pl.pallas_call(
        feed_kernel,
        grid=(tokens // BLOCK,),
        out_shape=[
            sds((tokens, D), jnp.bfloat16),
            sds((tokens, D), jnp.float32),
            sds((tokens, D), jnp.bfloat16),
        ]
        + [sds(w.shape, jnp.bfloat16) for w in weights]
        + [sds((1, D), jnp.float32)],
        in_specs=[rows, rows, rows, whole(gains.shape)] + [fixed(w.shape) for w in weights],
        out_specs=[rows, rows, rows] + [fixed(w.shape) for w in weights] + [whole((1, D))],
        scratch_shapes=[pltpu.VMEM(w.shape, jnp.float32) for w in weights],
        compiler_params=params(),
        cost_estimate=pl.CostEstimate(
            flops=60 * 10**9, bytes_accessed=30 * 10**6, transcendentals=3 * 10**6
        ),
        name="feed_forward",
    )(x, att, cot, gains, wo, wg, wu, wd)


def attention_backward(
    x, gains, seg_col, seg_row, cosine, sine, wq, wk, wv, q, k, v, lse, att_back, mid_back
):
    seqs, seq = x.shape[0], x.shape[1]
    return pl.pallas_call(
        attend_back_kernel,
        grid=(seqs,),
        out_shape=[sds(x.shape, jnp.float32)]
        + [sds(w.shape, jnp.bfloat16) for w in (wq, wk, wv)]
        + [sds((1, D), jnp.float32)],
        in_specs=[per_step(x.shape), whole(gains.shape)]
        + [per_step(a.shape) for a in (seg_col, seg_row, cosine, sine)]
        + [whole(w.shape) for w in (wq, wk, wv)]
        + [per_step(a.shape) for a in (q, k, v, lse, att_back, mid_back)],
        out_specs=[per_step(x.shape)] + [whole(w.shape) for w in (wq, wk, wv)] + [whole((1, D))],
        scratch_shapes=[
            pltpu.VMEM((HEADS, seq, HEAD), jnp.bfloat16),
            pltpu.VMEM((HEADS, seq, HEAD), jnp.float32),
            pltpu.VMEM((KV_HEADS, seq, HEAD), jnp.float32),
            pltpu.VMEM((KV_HEADS, seq, HEAD), jnp.float32),
            pltpu.VMEM((seq, BLOCK), jnp.float32),
        ]
        + [pltpu.VMEM(w.shape, jnp.float32) for w in (wq, wk, wv)],
        compiler_params=params(),
        cost_estimate=pl.CostEstimate(
            flops=120 * 10**9, bytes_accessed=40 * 10**6, transcendentals=2 * 10**7
        ),
        name="attention_backward",
    )(x, gains, seg_col, seg_row, cosine, sine, wq, wk, wv, q, k, v, lse, att_back, mid_back)


def gather_group(shards, shapes, count):
    packed = jnp.concatenate([shard.astype(jnp.bfloat16) for shard in shards])
    rows = lax.all_gather(packed, "dp", axis=0, tiled=False)
    result = []
    place = 0
    for shard, shape in zip(shards, shapes):
        size = shard.shape[0]
        result.append(rows[:, place : place + size].reshape(shape))
        place += size
    return result


def reduce_group(grads, sizes, count):
    total = sum(sizes)
    lanes = -(-total // 128)
    parts = [grad.reshape(count, size) for grad, size in zip(grads, sizes)]
    if lanes * 128 > total:
        parts.append(jnp.zeros((count, lanes * 128 - total), jnp.bfloat16))
    held = jnp.concatenate(parts, axis=1).reshape(count, lanes, 128)
    me = lax.axis_index("dp")
    bit = 1
    while bit < count:
        pairs = held.reshape(held.shape[0] // 2, 2, lanes, 128)
        mine = lax.rem(lax.div(me, bit), 2)
        keep = lax.dynamic_index_in_dim(pairs, mine, 1, keepdims=False)
        give = lax.dynamic_index_in_dim(pairs, 1 - mine, 1, keepdims=False)
        got = lax.ppermute(give, "dp", [(d, d ^ bit) for d in range(count)])
        held = keep.astype(jnp.float32) + got.astype(jnp.float32)
        bit *= 2
        if bit < count:
            held = held.astype(jnp.bfloat16)
    flat = held.reshape(-1)
    result = []
    place = 0
    for size in sizes:
        result.append(flat[place : place + size])
        place += size
    return result


def butterfly(values, count):
    bit = 1
    while bit < count:
        values = values + lax.ppermute(values, "dp", [(d, d ^ bit) for d in range(count)])
        bit *= 2
    return values


def adam_step(weight_now, gradient, moment_one, moment_two, step_rate, decay_value):
    one_new = beta_first * moment_one + (1.0 - beta_first) * gradient
    two_new = beta_second * moment_two + (1.0 - beta_second) * gradient * gradient
    fix_first = 1.0 - beta_first**STEP
    fix_second = 1.0 - beta_second**STEP
    weight_new = weight_now - step_rate * (
        one_new / fix_first / (jnp.sqrt(two_new / fix_second) + adam_eps) + decay_value * weight_now
    )
    return (two_new, weight_new)


def body(count, inputs, cotangent, segments, norm_gains, *rest):
    masters, firsts, seconds = rest[0:7], rest[7:14], rest[14:21]
    gain_first, gain_second = rest[21:23]
    query_cols = HEADS * HEAD
    pair_cols = KV_HEADS * HEAD
    shapes = (
        (D, query_cols),
        (D, pair_cols),
        (D, pair_cols),
        (query_cols, D),
        (D, FF),
        (D, FF),
        (FF, D),
    )
    sizes = [master.shape[0] for master in masters]
    seqs, seq = inputs.shape[0], inputs.shape[1]
    wq, wk, wv = gather_group(masters[:3], shapes[:3], count)
    wo, wg, wu, wd = gather_group(masters[3:], shapes[3:], count)
    cosine, sine = rope_tables(doc_positions(segments))
    seg_col, seg_row = segments[:, :, None], segments[:, None, :]
    common = (inputs, norm_gains, seg_col, seg_row, cosine, sine, wq, wk, wv)
    q, k, v, lse, att = attention_forward(*common)
    flat = (seqs * seq, D)
    out, mid_back, att_back, grad_o, grad_g, grad_u, grad_d, gain_two = feed_forward(
        inputs.reshape(flat), att.reshape(flat), cotangent.reshape(flat), norm_gains, wo, wg, wu, wd
    )
    late = reduce_group((grad_o, grad_g, grad_u, grad_d), sizes[3:], count)
    whole_shape = inputs.shape
    x_back, grad_q, grad_k, grad_v, gain_one = attention_backward(
        *common, q, k, v, lse, att_back.reshape(whole_shape), mid_back.reshape(whole_shape)
    )
    early = reduce_group((grad_q, grad_k, grad_v), sizes[:3], count)
    gain_sum = jnp.concatenate([butterfly(gain_one, count), butterfly(gain_two, count)], axis=0)
    results = [out.reshape(whole_shape), x_back]
    for slot_index, gradient in enumerate(early + late):
        moment_new, weight_new = adam_step(
            masters[slot_index],
            gradient,
            firsts[slot_index],
            seconds[slot_index],
            learn_rate,
            decay_rate,
        )
        results.extend([gradient, moment_new, weight_new])
    gain_moment, gains_new = adam_step(
        norm_gains, gain_sum, gain_first, gain_second, gain_rate, 0.0
    )
    results.extend([gain_sum, gain_moment, gains_new])
    return tuple(results)


def solution(mesh):
    rows = P("dp", None, None)
    in_specs = (rows, rows, P("dp", None), P()) + (P("dp"),) * 21 + (P(), P())
    out_specs = (rows, rows) + (P("dp"),) * 21 + (P(), P(), P())
    return jax.shard_map(
        functools.partial(body, mesh.shape["dp"]),
        mesh=mesh,
        in_specs=in_specs,
        out_specs=out_specs,
        check_vma=False,
    )
```
